32 devices in a mesh: gx: 2 (over x), gy: 4 (over y, core), gz: 4 (over z).
Axes of the slice: x: 2, y: 2, z: 4, core: 2. Of those that a mesh axis runs over, the one named last changes fastest.
Arguments:
- right_side: float32 [3, 16, 32, 32, 128], P(None, 'gx', 'gy', 'gz'), may hold values from -24 to 24
- stiffness: float32 [3, 16, 32, 32], P(None, 'gx', 'gy', 'gz'), may hold values from 0.25 to 4
- local_factor: bfloat16 [2, 4, 4, 2048, 2048], P('gx', 'gy', 'gz'), as said below
- basis: bfloat16 [2, 4, 4, 64, 1536], P('gx', 'gy', 'gz'), may hold values from -0.3125 to 0.3125
- coarse_map: int32 [2, 4, 4, 64], P('gx', 'gy', 'gz'), may hold values from 0 to 63, each once within a row
- margin_index: int32 [2, 4, 4, 512], P('gx', 'gy', 'gz'), may hold values from 0 to 1151, as said below
- coarse_inverse: bfloat16 [2048, 2048], P(('gx', 'gy', 'gz')), as said below
Outputs:
- solution: float32 [3, 16, 32, 32, 128], P(None, 'gx', 'gy', 'gz')
- residual_ratio: float32 [128], replicated
The draws below stay inside these ranges and needn't reach their ends.
Inputs may be any that keep to these rules, and one draw needn't show every extreme that they name: `local_factor`: each subdomain's factor is zero above its diagonal. coarse_inverse is symmetric. `margin_index`: within each subdomain the 512 entries are distinct and increasing. `coarse_map`: each subdomain's entries are a permutation of 0 to 63.
All inputs are finite; a program needn't handle non-finite values.
Results may differ from the reference program's by a relative error of at most 0.0055.
Values may be sent and summed in bfloat16 or wider, within the bound.
A program may use at most 64 MiB of HBM per device.

```python
import math
import jax
import jax.numpy as jnp
from jax import lax

CX = 8
CY = 8
CZ = 8
R = 128
LOC = 2048
CB = 64
OWN = 1536
OVL = 512
HALO_DOFS = 1152
COARSE = 2048
NX = 16
NY = 32
NZ = 32
N_GX = 2
N_GY = 4
N_GZ = 4


def draw_local_factor(key, part):
    sub_count = NX // CX * (NY // CY) * (NZ // CZ)
    sub_keys = jax.random.split(key, sub_count)
    row_ids = lax.broadcasted_iota(jnp.int32, (LOC, LOC), 0)
    col_ids = lax.broadcasted_iota(jnp.int32, (LOC, LOC), 1)

    def one_factor(sub_key):
        key_low, key_high = jax.random.split(sub_key)
        spread = jax.random.normal(key_low, (LOC, LOC), jnp.float32)
        diagonal = jax.random.uniform(key_high, (LOC,), jnp.float32, 0.75, 1.25)
        below = jnp.where(col_ids < row_ids, spread * (0.6 / math.sqrt(LOC)), 0.0)
        return (below + jnp.where(col_ids == row_ids, diagonal[:, None], 0.0)).astype(jnp.bfloat16)
    return lax.map(one_factor, sub_keys).reshape(NX // CX, NY // CY, NZ // CZ, LOC, LOC)


def draw_margin_index(key, part):
    sub_count = NX // CX * (NY // CY) * (NZ // CZ)
    sub_keys = jax.random.split(key, sub_count)

    def one_choice(sub_key):
        shuffled = jax.random.permutation(sub_key, HALO_DOFS - 2) + 1
        chosen = jnp.sort(shuffled[:OVL - 2]).astype(jnp.int32)
        return jnp.concatenate([jnp.zeros((1,), jnp.int32), chosen, jnp.full((1,), HALO_DOFS - 1, jnp.int32)])
    return jax.vmap(one_choice)(sub_keys).reshape(NX // CX, NY // CY, NZ // CZ, OVL)


def draw_coarse_inverse(key, part):
    key_low, key_high = jax.random.split(key)
    raw_draw = jax.random.normal(key_low, (COARSE, COARSE), jnp.float32)
    row_ids = lax.broadcasted_iota(jnp.int32, (COARSE, COARSE), 0)
    col_ids = lax.broadcasted_iota(jnp.int32, (COARSE, COARSE), 1)
    symmetric = (raw_draw + raw_draw.T) * (0.4 / math.sqrt(2.0 * COARSE))
    diagonal = jax.random.uniform(key_high, (COARSE,), jnp.float32, 0.8, 1.2)
    return (symmetric + jnp.where(row_ids == col_ids, diagonal[:, None], 0.0)).astype(jnp.bfloat16)


def block_levels(key, extent, shards, low, top_value):
    def one(axis_at, parts):
        draws = jax.random.uniform(jax.random.fold_in(jax.random.fold_in(key, 6), axis_at), (parts,), jnp.float32, low / len(shards), top_value / len(shards))
        return jnp.repeat(jnp.exp(draws), extent[axis_at] // parts).reshape((-1,) + (1,) * (len(extent) - axis_at - 1))

    gain = one(*shards[0])
    for cut in shards[1:]:
        gain = gain * one(*cut)
    return gain


def normal_values(own_key, dims, scale, bound, cuts=(), kind=jnp.bfloat16):
    level = block_levels(own_key, dims, cuts, -0.22, 0.18) if cuts else 1.0
    entries = jax.random.normal(own_key, dims, jnp.float32) * scale * level
    return jnp.minimum(jnp.maximum(entries, -bound), bound).astype(kind)


def setup_inputs(seed: int = 0) -> dict:
    arg_keys = jax.random.split(jax.random.key(seed), 8)
    return {
        "right_side": normal_values(arg_keys[0], (3, NX, NY, NZ, R), 4.0, 24.0, ((1, 2), (2, 4), (3, 4)), jnp.float32),
        "stiffness": jnp.clip(jnp.exp(math.log(4.0) - 2.7725887 * jax.random.uniform(arg_keys[1], (3, NX, NY, NZ), jnp.float32) ** block_levels(arg_keys[1], (3, NX, NY, NZ), ((1, 2), (2, 4), (3, 4)), -0.2, 0.2)), 0.25, 4.0),
        "local_factor": draw_local_factor(jax.random.fold_in(arg_keys[7], 71), 0),
        "basis": normal_values(arg_keys[3], (N_GX, N_GY, N_GZ, CB, OWN), (OWN // 4) ** -0.5, 0.3125, ((0, 2), (1, 4), (2, 4))),
        "coarse_map": jax.vmap(lambda own: jax.random.permutation(own, CB))(jax.random.split(arg_keys[4], N_GX * N_GY * N_GZ)).reshape((N_GX, N_GY, N_GZ, CB)).astype(jnp.int32),
        "margin_index": draw_margin_index(jax.random.fold_in(arg_keys[7], 71), 0),
        "coarse_inverse": draw_coarse_inverse(jax.random.fold_in(arg_keys[7], 71), 0),
    }


EPSILON = 1e-06

def inner(left, right):
    return lax.optimization_barrier(jnp.sum(left * right, axis=(0, 1, 2, 3)))

def face_rows(padded):
    rhs_count = padded.shape[-1]
    slabs = [padded[:, 0, 1:-1, 1:-1], padded[:, -1, 1:-1, 1:-1], padded[:, 1:-1, 0, 1:-1], padded[:, 1:-1, -1, 1:-1], padded[:, 1:-1, 1:-1, 0], padded[:, 1:-1, 1:-1, -1]]
    joined = jnp.concatenate([slab.reshape(slab.shape[0], -1, rhs_count) for slab in slabs], axis=1)
    return joined.reshape(-1, rhs_count)

def operate(field, stiffness):
    padded = jnp.pad(field, ((0, 0), (1, 1), (1, 1), (1, 1), (0, 0)))
    beside = padded[:, 2:, 1:-1, 1:-1] + padded[:, :-2, 1:-1, 1:-1]
    beside = beside + padded[:, 1:-1, 2:, 1:-1] + padded[:, 1:-1, :-2, 1:-1]
    beside = beside + padded[:, 1:-1, 1:-1, 2:] + padded[:, 1:-1, 1:-1, :-2]
    return (6.0 + stiffness[..., None]) * field - beside

def reference(right_side, stiffness, local_factor, basis, coarse_map, margin_index, coarse_inverse):
    x_parts = NX // CX
    y_parts = NY // CY
    z_parts = NZ // CZ
    devices = x_parts * y_parts * z_parts
    factors = local_factor.reshape(devices, LOC, LOC)
    bases = basis.reshape(devices, CB, OWN)
    coarse_maps = coarse_map.reshape(devices, CB).astype(jnp.int32)
    margin_picks = margin_index.reshape(devices, OVL).astype(jnp.int32)
    offsets = jnp.arange(devices, dtype=jnp.int32) * CB
    targets = (offsets[:, None] + coarse_maps).astype(jnp.int32)
    device_ids = jnp.arange(devices, dtype=jnp.int32)

    def to_blocks(field):
        shaped = field.reshape(3, x_parts, CX, y_parts, CY, z_parts, CZ, R)
        return shaped.transpose(1, 3, 5, 0, 2, 4, 6, 7).reshape(devices, OWN, R)

    def from_blocks(blocks):
        shaped = blocks.reshape(x_parts, y_parts, z_parts, 3, CX, CY, CZ, R)
        return shaped.transpose(3, 0, 4, 1, 5, 2, 6, 7).reshape(3, NX, NY, NZ, R)

    def precondition(field):
        rounded = field.astype(jnp.bfloat16)
        padded = jnp.pad(rounded, ((0, 0), (1, 1), (1, 1), (1, 1), (0, 0)))
        own_all = to_blocks(rounded)

        def local_solve(device_index):
            x_index = device_index // (y_parts * z_parts)
            y_index = device_index // z_parts % y_parts
            z_index = device_index % z_parts
            anchor = jnp.int32(0)
            block = lax.dynamic_slice(padded, (anchor, (x_index * CX).astype(jnp.int32), (y_index * CY).astype(jnp.int32), (z_index * CZ).astype(jnp.int32), anchor), (3, CX + 2, CY + 2, CZ + 2, R))
            own_rows = own_all[device_index]
            extended = jnp.concatenate([own_rows, jnp.take(face_rows(block), margin_picks[device_index], axis=0)], axis=0)
            factor = factors[device_index]
            front_values = jnp.dot(factor, extended, preferred_element_type=jnp.float32).astype(jnp.bfloat16)
            back_sweep = jnp.dot(factor.T, front_values, preferred_element_type=jnp.float32)[:OWN]
            restricted = jnp.dot(bases[device_index], own_rows, preferred_element_type=jnp.float32)
            return (back_sweep, restricted)
        local_parts, restricted = lax.map(local_solve, device_ids)
        coarse_residual = jnp.zeros((COARSE, R), jnp.float32).at[targets.reshape(-1)].set(restricted.reshape(-1, R)).astype(jnp.bfloat16)
        coarse_solution = jnp.dot(coarse_inverse, coarse_residual, preferred_element_type=jnp.float32).astype(jnp.bfloat16)
        picked = coarse_solution[targets]

        def prolong(device_index):
            return jnp.dot(bases[device_index].T, picked[device_index], preferred_element_type=jnp.float32)
        coarse_parts = lax.map(prolong, device_ids)
        return from_blocks(local_parts + coarse_parts)
    start_norm = jnp.sqrt(inner(right_side, right_side) + EPSILON)
    basis_one = right_side / start_norm
    search_one = precondition(basis_one)
    image_one = operate(search_one, stiffness)
    along_one = inner(image_one, basis_one)
    rest_one = image_one - along_one * basis_one
    norm_two = jnp.sqrt(inner(rest_one, rest_one) + EPSILON)
    basis_two = rest_one / norm_two
    search_two = precondition(basis_two)
    image_two = operate(search_two, stiffness)
    cross_two = inner(image_two, basis_one)
    along_two = inner(image_two, basis_two)
    rest_two = image_two - cross_two * basis_one - along_two * basis_two
    norm_three = jnp.sqrt(inner(rest_two, rest_two) + EPSILON)
    radius_one = jnp.sqrt(along_one * along_one + norm_two * norm_two)
    cosine_one = along_one / radius_one
    sine_one = norm_two / radius_one
    turned_one = cosine_one * cross_two + sine_one * along_two
    turned_two = cosine_one * along_two - sine_one * cross_two
    radius_two = jnp.sqrt(turned_two * turned_two + norm_three * norm_three)
    cosine_two = turned_two / radius_two
    sine_two = norm_three / radius_two
    coef_two = -cosine_two * sine_one * start_norm / radius_two
    coef_one = (cosine_one * start_norm - turned_one * coef_two) / radius_one
    solution = coef_one * search_one + coef_two * search_two
    return (solution, sine_one * sine_two)
```

```python
import functools
import jax
import jax.numpy as jnp
from jax import lax
from jax.experimental import pallas as pl
from jax.experimental.pallas import tpu as pltpu
from jax.sharding import PartitionSpec as P

EPSILON = 1e-06
AXES = ("gx", "gy", "gz")
MESH = pl.DeviceIdType.MESH
F32 = jnp.float32
BF16 = jnp.bfloat16


def dot(a, b):
    return jnp.dot(a, b, preferred_element_type=F32)


def kernel(
    dims,
    cells,
    right_hbm,
    stiff_ref,
    factor_hbm,
    basis_hbm,
    map_ref,
    margin_ref,
    inverse_hbm,
    solution_ref,
    ratio_ref,
    right,
    factor,
    basis,
    inverse,
    own,
    placed_basis,
    onehot,
    face_factor,
    diagonal,
    search,
    image,
    zpad,
    front,
    back,
    send_faces,
    faces,
    coarse,
    sums_z,
    sums_xy,
    load_sem,
    factor_sem,
    face_send,
    face_recv,
    coarse_send,
    coarse_recv,
    sum_send,
    sum_recv,
):
    count_x, count_y, count_z = dims
    comps, cx, cy, cz = cells
    plane = cy * cz
    slab = cx * plane
    rows = comps * slab
    size = factor.shape[0]
    blk = 256
    own_blocks, all_blocks = rows // blk, size // blk
    gx, gy, gz = (lax.axis_index(axis) for axis in AXES)
    low_count = coarse.shape[3]
    high_count = count_y // low_count
    gy_high, gy_low = lax.div(gy, low_count), lax.rem(gy, low_count)
    plane_id = gx * count_y + gy

    loads = [
        pltpu.make_async_copy(src, dst, load_sem.at[i])
        for i, (src, dst) in enumerate(
            [(right_hbm, right), (basis_hbm, basis), (inverse_hbm, inverse)]
        )
    ]
    loads[0].start()
    loads[1].start()
    factor_loads = []
    for i in range(all_blocks):
        part = (pl.ds(i * blk, blk), pl.ds(0, (i + 1) * blk))
        factor_loads.append(
            pltpu.make_async_copy(factor_hbm.at[part], factor.at[part], factor_sem.at[i])
        )
        factor_loads[-1].start()
    loads[2].start()

    barrier = pltpu.get_barrier_semaphore()
    z_peers = [{"gz": lax.rem(gz + d, count_z)} for d in range(1, count_z)]
    xy_peers = []
    for d in range(1, count_x * count_y):
        other = lax.rem(plane_id + d, count_x * count_y)
        xy_peers.append({"gx": lax.div(other, count_y), "gy": lax.rem(other, count_y)})
    for peer in z_peers + xy_peers:
        pl.semaphore_signal(barrier, inc=1, device_id=peer, device_id_type=MESH)

    here = (gx, gx, gy, gy, gz, gz)
    counts = (count_x, count_x, count_y, count_y, count_z, count_z)
    present = [
        here[f] > 0 if f % 2 == 0 else here[f] < counts[f] - 1 for f in range(6)
    ]
    for f in range(6):

        @pl.when(jnp.logical_not(present[f]))
        def _():
            for e in range(4):
                faces[e, f] = jnp.zeros(faces.shape[2:], BF16)

    eye = lax.broadcasted_iota(jnp.int32, (cz, cz), 0) == lax.broadcasted_iota(
        jnp.int32, (cz, cz), 1
    )

    def fill(i, carry):
        tile = stiff_ref[i]
        for y in range(cy):
            line = jnp.sum(jnp.where(eye, tile[y : y + 1, :], 0.0), axis=1, keepdims=True)
            start = pl.multiple_of(i * plane + y * cz, cz)
            diagonal[pl.ds(start, cz), :] = jnp.broadcast_to(line + 6.0, (cz, right.shape[1]))
        return carry

    lax.fori_loop(0, comps * cx, fill, 0)

    margin = margin_ref[...]
    for f in range(6):
        for c in range(comps):
            ids = lax.broadcasted_iota(jnp.int32, (plane, margin.shape[1]), 0) + (
                (c * 6 + f) * plane
            )
            onehot[pl.ds((f * comps + c) * plane, plane), :] = jnp.where(
                ids == margin, 1.0, 0.0
            ).astype(BF16)

    def face_copy(e, f):
        step = 1 if f % 2 else -1
        axis = AXES[f // 2]
        return pltpu.make_async_remote_copy(
            src_ref=send_faces.at[e, f],
            dst_ref=faces.at[e, f ^ 1],
            send_sem=face_send.at[e, f],
            recv_sem=face_recv.at[e, f ^ 1],
            device_id={axis: here[f] + step},
            device_id_type=MESH,
        )

    def face_arrival(e, f):
        return pltpu.make_async_remote_copy(
            src_ref=send_faces.at[e, f],
            dst_ref=faces.at[e, f],
            send_sem=face_send.at[e, f],
            recv_sem=face_recv.at[e, f],
            device_id={AXES[f // 2]: here[f]},
            device_id_type=MESH,
        )

    def pack_faces(e, field):
        for f in range(6):
            for c in range(comps):
                base = c * slab
                if f < 2:
                    x = 0 if f == 0 else cx - 1
                    piece = field[pl.ds(base + x * plane, plane), :]
                elif f < 4:
                    y = 0 if f == 2 else cy - 1
                    piece = jnp.concatenate(
                        [field[pl.ds(base + x * plane + y * cz, cz), :] for x in range(cx)], axis=0
                    )
                else:
                    z = 0 if f == 4 else cz - 1
                    piece = field[pl.ds(base + z, cx * cy, stride=cz), :]
                send_faces[e, f, pl.ds(c * plane, plane), :] = piece.astype(BF16)

            @pl.when(present[f])
            def _():
                face_copy(e, f).start()

    def wait_faces(e):
        for f in range(6):

            @pl.when(present[f])
            def _():
                face_arrival(e, f).wait_recv()

    def coarse_stages(k):
        def copy(view, peer, number):
            return pltpu.make_async_remote_copy(
                src_ref=view,
                dst_ref=view,
                send_sem=coarse_send.at[k, number],
                recv_sem=coarse_recv.at[k, number],
                device_id=peer,
                device_id_type=MESH,
            )

        stages, number = [], 0
        plan = [
            (coarse.at[k, gx, gy_high, gy_low, gz], count_z, lambda d: {"gz": lax.rem(gz + d, count_z)}),
            (coarse.at[k, gx, gy_high, gy_low], count_x, lambda d: {"gx": lax.rem(gx + d, count_x)}),
            (
                coarse.at[k, :, gy_high, gy_low],
                high_count,
                lambda d: {"gy": lax.rem(gy_high + d, high_count) * low_count + gy_low},
            ),
            (
                coarse.at[k, :, :, gy_low],
                low_count,
                lambda d: {"gy": gy_high * low_count + lax.rem(gy_low + d, low_count)},
            ),
        ]
        for view, count, peer in plan:
            stage = []
            for d in range(1, count):
                stage.append(copy(view, peer(d), number))
                number += 1
            stages.append(stage)
        return stages

    def start(stage):
        for copy in stage:
            copy.start()

    def arrive(stage):
        for copy in stage:
            copy.wait_recv()

    every_stage = []

    def precondition(k, e):
        residual = dot(placed_basis[...], own[...]).astype(BF16)
        coarse[k, gx, gy_high, gy_low, gz] = residual
        stages = coarse_stages(k)
        every_stage.extend(stages)
        start(stages[0])
        for i in range(own_blocks):
            if k == 0:
                factor_loads[i].wait()
            values = dot(factor[pl.ds(i * blk, blk), pl.ds(0, (i + 1) * blk)], own[pl.ds(0, (i + 1) * blk), :])
            front[:, pl.ds(i * blk, blk)] = values.T.astype(BF16)
        arrive(stages[0])
        start(stages[1])
        for j in range(own_blocks):
            back[:, pl.ds(j * blk, blk)] = dot(
                front[:, pl.ds(j * blk, rows - j * blk)],
                factor[pl.ds(j * blk, rows - j * blk), pl.ds(j * blk, blk)],
            )
        arrive(stages[1])
        start(stages[2])
        if k == 0:
            for i in range(own_blocks, all_blocks):
                factor_loads[i].wait()
                wide = (i + 1) * blk - rows
                face_factor[pl.ds(i * blk - rows, blk), :] = lax.dot_general(
                    factor[pl.ds(i * blk, blk), pl.ds(rows, wide)],
                    onehot[:, pl.ds(0, wide)],
                    (((1,), (1,)), ((), ())),
                    preferred_element_type=F32,
                ).astype(BF16)
        wait_faces(e)
        margin_faces = faces[e].reshape(-1, faces.shape[-1])
        for i in range(own_blocks, all_blocks):
            values = dot(factor[pl.ds(i * blk, blk), pl.ds(0, rows)], own[...]) + dot(
                face_factor[pl.ds(i * blk - rows, blk), :], margin_faces
            )
            front[:, pl.ds(i * blk, blk)] = values.T.astype(BF16)
        arrive(stages[2])
        start(stages[3])
        for j in range(own_blocks):
            back[:, pl.ds(j * blk, blk)] += dot(
                front[:, pl.ds(rows, size - rows)],
                factor[pl.ds(rows, size - rows), pl.ds(j * blk, blk)],
            )
        if k == 0:
            loads[2].wait()
        arrive(stages[3])
        solved = dot(inverse[...], coarse[k].reshape(-1, coarse.shape[-1]))
        solved = solved.T.astype(BF16)
        for j in range(own_blocks):
            cut = pl.ds(j * blk, blk)
            search[k, cut, :] = (back[:, cut] + dot(solved, placed_basis[:, cut])).T

    def operate(k, e):
        field = search.at[k]
        wait_faces(e)
        zi = lax.broadcasted_iota(jnp.int32, (cy, cz, right.shape[1]), 1)
        totals = None
        for c in range(comps):
            base = c * slab
            cut = pl.ds(c * plane, plane)
            x_low, x_high, y_low, y_high, z_low, z_high = (
                faces[e, f, cut, :].astype(F32) for f in range(6)
            )
            zpad[pl.ds(base, cx * cy, stride=cz), :] = z_low
            zpad[pl.ds(base + cz - 1, cx * cy, stride=cz), :] = z_high
            for x in range(cx):
                at = pl.ds(base + x * plane, plane)
                flat = field[at, :]
                center = flat.reshape(cy, cz, -1)
                lower = field[pl.ds(base + (x - 1) * plane, plane), :] if x else x_low
                upper = field[pl.ds(base + (x + 1) * plane, plane), :] if x < cx - 1 else x_high
                edge = zpad[at, :].reshape(cy, cz, -1)
                beside = (lower + upper).reshape(cy, cz, -1)
                beside += jnp.concatenate([y_low[x * cz : (x + 1) * cz][None], center[:-1]], axis=0)
                beside += jnp.concatenate([center[1:], y_high[x * cz : (x + 1) * cz][None]], axis=0)
                beside += jnp.where(zi == 0, edge, pltpu.roll(center, 1, axis=1))
                beside += jnp.where(zi == cz - 1, edge, pltpu.roll(center, cz - 1, axis=1))
                out = diagonal[at, :].reshape(cy, cz, -1) * center - beside
                given = right[at, :].reshape(cy, cz, -1)
                if k == 0:
                    flat_out = out.reshape(plane, -1)
                    image[at, :] = flat_out
                    own[at, :] = flat_out.astype(BF16)
                    terms = [given * given, out * given, out * out]
                else:
                    first = image[at, :].reshape(cy, cz, -1)
                    terms = [out * given, out * first, out * out]
                terms = [jnp.sum(term, axis=0) for term in terms]
                totals = terms if totals is None else [a + b for a, b in zip(totals, terms)]
        for q, total in enumerate(totals):
            sums_z[gz, pl.ds(k * 3 + q, 1), :] = jnp.sum(total, axis=0, keepdims=True)

    sums_z[gz] = jnp.zeros(sums_z.shape[1:], F32)
    loads[1].wait()
    ids = lax.broadcasted_iota(jnp.int32, (basis.shape[0], basis.shape[0]), 0)
    table = jnp.where(ids == map_ref[...], 1.0, 0.0).astype(BF16)
    placed_basis[...] = dot(table, basis[...]).astype(BF16)
    loads[0].wait()
    own[...] = right[...].astype(BF16)
    pl.semaphore_wait(barrier, len(z_peers) + len(xy_peers))
    pack_faces(0, right)
    precondition(0, 0)
    pack_faces(1, search.at[0])
    operate(0, 1)
    pack_faces(2, image)
    precondition(1, 2)
    pack_faces(3, search.at[1])
    operate(1, 3)

    sum_copies = []

    def share(slots, index, peers, base):
        copies = []
        for n, peer in enumerate(peers):
            copies.append(
                pltpu.make_async_remote_copy(
                    src_ref=slots.at[index],
                    dst_ref=slots.at[index],
                    send_sem=sum_send.at[base + n],
                    recv_sem=sum_recv.at[base + n],
                    device_id=peer,
                    device_id_type=MESH,
                )
            )
        start(copies)
        arrive(copies)
        sum_copies.extend(copies)
        total = slots[0]
        for n in range(1, slots.shape[0]):
            total = total + slots[n]
        return total

    sums_xy[plane_id] = share(sums_z, gz, z_peers, 0)
    total = share(sums_xy, plane_id, xy_peers, len(z_peers))
    vv, iv, ii, tv, ti, tt = (total[q : q + 1] for q in range(6))

    start_square = vv + EPSILON
    start_norm = jnp.sqrt(start_square)
    along_one = iv / start_square
    rest = jnp.maximum(
        ii / start_square - along_one * along_one * (2.0 - vv / start_square), 0.0
    )
    square_two = rest + EPSILON
    norm_two = jnp.sqrt(square_two)
    scale = start_norm * norm_two
    cross_two = (tv - along_one * iv) / (start_square * norm_two)
    along_two = (ti - along_one * ii - along_one * (tv - along_one * iv)) / (
        start_square * square_two
    )
    square_image = (tt - along_one * (2.0 * ti - along_one * ii)) / (start_square * square_two)
    overlap = (iv - along_one * vv) / (start_square * norm_two)
    rest = (
        square_image
        - cross_two * cross_two * (2.0 - vv / start_square)
        - along_two * along_two * (2.0 - rest / square_two)
        + 2.0 * cross_two * along_two * overlap
    )
    norm_three = jnp.sqrt(jnp.maximum(rest, 0.0) + EPSILON)
    radius_one = jnp.sqrt(along_one * along_one + square_two)
    cosine_one = along_one / radius_one
    sine_one = norm_two / radius_one
    turned_one = cosine_one * cross_two + sine_one * along_two
    turned_two = cosine_one * along_two - sine_one * cross_two
    radius_two = jnp.sqrt(turned_two * turned_two + norm_three * norm_three)
    cosine_two = turned_two / radius_two
    sine_two = norm_three / radius_two
    coef_two = -cosine_two * sine_one * start_norm / radius_two
    coef_one = (cosine_one * start_norm - turned_one * coef_two) / radius_one
    ratio_ref[...] = sine_one * sine_two
    weight_two = coef_two / scale
    weight_one = coef_one / start_norm - along_one * weight_two
    solution_ref[...] = weight_one * search[0] + weight_two * search[1]

    for stage in every_stage + [sum_copies]:
        for copy in stage:
            copy.wait_send()
    for e in range(4):
        for f in range(6):

            @pl.when(present[f])
            def _():
                face_copy(e, f).wait_send()


def local(dims, right_side, stiffness, local_factor, basis, coarse_map, margin_index, coarse_inverse):
    cells = right_side.shape[:4]
    comps, cx, cy, cz = cells
    rhs = right_side.shape[-1]
    rows = comps * cx * cy * cz
    size = local_factor.shape[-1]
    functions = basis.shape[-2]
    margin = margin_index.shape[-1]
    face = comps * cy * cz
    assert cx == cy == cz and rows % 256 == 0 and size % 256 == 0
    low_count = 2 if dims[1] % 2 == 0 else 1
    devices = dims[0] * dims[1] * dims[2]
    copies = sum(n - 1 for n in (dims[2], dims[0], dims[1] // low_count, low_count))
    sum_copies = dims[2] - 1 + dims[0] * dims[1] - 1
    anywhere = pl.BlockSpec(memory_space=pl.ANY)
    vmem = pl.BlockSpec(memory_space=pltpu.VMEM)
    solved, ratio = pl.pallas_call(
        functools.partial(kernel, dims, cells),
        out_shape=(
            jax.ShapeDtypeStruct((rows, rhs), F32),
            jax.ShapeDtypeStruct((1, rhs), F32),
        ),
        in_specs=[anywhere, vmem, anywhere, anywhere, vmem, vmem, anywhere],
        out_specs=(vmem, vmem),
        scratch_shapes=[
            pltpu.VMEM((rows, rhs), F32),
            pltpu.VMEM((size, size), BF16),
            pltpu.VMEM((functions, rows), BF16),
            pltpu.VMEM(coarse_inverse.shape, BF16),
            pltpu.VMEM((rows, rhs), BF16),
            pltpu.VMEM((functions, rows), BF16),
            pltpu.VMEM((6 * face, margin), BF16),
            pltpu.VMEM((margin, 6 * face), BF16),
            pltpu.VMEM((rows, rhs), F32),
            pltpu.VMEM((2, rows, rhs), F32),
            pltpu.VMEM((rows, rhs), F32),
            pltpu.VMEM((rows, rhs), F32),
            pltpu.VMEM((rhs, size), BF16),
            pltpu.VMEM((rhs, rows), F32),
            pltpu.VMEM((4, 6, face, rhs), BF16),
            pltpu.VMEM((4, 6, face, rhs), BF16),
            pltpu.VMEM(
                (2, dims[0], dims[1] // low_count, low_count, dims[2], functions, rhs), BF16
            ),
            pltpu.VMEM((dims[2], 8, rhs), F32),
            pltpu.VMEM((dims[0] * dims[1], 8, rhs), F32),
            pltpu.SemaphoreType.DMA((3,)),
            pltpu.SemaphoreType.DMA((size // 256,)),
            pltpu.SemaphoreType.DMA((4, 6)),
            pltpu.SemaphoreType.DMA((4, 6)),
            pltpu.SemaphoreType.DMA((2, copies)),
            pltpu.SemaphoreType.DMA((2, copies)),
            pltpu.SemaphoreType.DMA((sum_copies,)),
            pltpu.SemaphoreType.DMA((sum_copies,)),
        ],
        compiler_params=pltpu.CompilerParams(
            collective_id=0, has_side_effects=True, vmem_limit_bytes=56 * 1024 * 1024
        ),
    )(
        right_side.reshape(rows, rhs),
        stiffness.reshape(comps * cx, cy, cz),
        local_factor.reshape(size, size),
        basis.reshape(functions, rows),
        coarse_map.reshape(1, functions),
        margin_index.reshape(1, margin),
        coarse_inverse,
    )
    return solved.reshape(right_side.shape), ratio.reshape(rhs)


def solution(mesh):
    dims = tuple(mesh.shape[axis] for axis in AXES)
    return jax.shard_map(
        functools.partial(local, dims),
        mesh=mesh,
        in_specs=(
            P(None, "gx", "gy", "gz", None),
            P(None, "gx", "gy", "gz"),
            P("gx", "gy", "gz", None, None),
            P("gx", "gy", "gz", None, None),
            P("gx", "gy", "gz", None),
            P("gx", "gy", "gz", None),
            P(("gx", "gy", "gz"), None),
        ),
        out_specs=(P(None, "gx", "gy", "gz", None), P()),
        check_vma=False,
    )
```

```python
import functools
import jax
import jax.numpy as jnp
from jax import lax
from jax.experimental import pallas as pl
from jax.experimental.pallas import tpu as pltpu
from jax.sharding import PartitionSpec as P

EPSILON = 1e-06
AXES = ("gx", "gy", "gz")
MESH = pl.DeviceIdType.MESH
F32 = jnp.float32
BF16 = jnp.bfloat16


def dot(a, b):
    return jnp.dot(a, b, preferred_element_type=F32)


def kernel(
    dims,
    cells,
    right_hbm,
    stiff_ref,
    factor_hbm,
    basis_hbm,
    map_ref,
    margin_ref,
    inverse_hbm,
    search_one_hbm,
    search_two_hbm,
    weights_ref,
    right,
    factor,
    basis,
    inverse,
    own,
    placed_basis,
    placed_turned,
    onehot,
    face_factor,
    diagonal,
    search,
    images,
    front,
    back,
    send_faces,
    faces,
    coarse,
    sums_z,
    sums_xy,
    load_sem,
    factor_sem,
    face_send,
    face_recv,
    coarse_send,
    coarse_recv,
    sum_send,
    sum_recv,
    out_sem,
):
    count_x, count_y, count_z = dims
    comps, cx, cy, cz = cells
    plane = cy * cz
    slab = cx * plane
    rows = comps * slab
    size = factor.shape[0]
    blk = 256
    own_blocks, all_blocks = rows // blk, size // blk
    gx, gy, gz = (lax.axis_index(axis) for axis in AXES)
    low_count = coarse.shape[3]
    high_count = count_y // low_count
    gy_high, gy_low = lax.div(gy, low_count), lax.rem(gy, low_count)
    plane_id = gx * count_y + gy

    loads = [
        pltpu.make_async_copy(src, dst, load_sem.at[i])
        for i, (src, dst) in enumerate(
            [(right_hbm, right), (basis_hbm, basis), (inverse_hbm, inverse)]
        )
    ]
    loads[0].start()
    loads[1].start()
    factor_loads = []
    for i in range(all_blocks):
        part = (pl.ds(i * blk, blk), pl.ds(0, (i + 1) * blk))
        factor_loads.append(
            pltpu.make_async_copy(factor_hbm.at[part], factor.at[part], factor_sem.at[i])
        )
        factor_loads[-1].start()
    loads[2].start()

    barrier = pltpu.get_barrier_semaphore()
    z_peers = [{"gz": lax.rem(gz + d, count_z)} for d in range(1, count_z)]
    xy_peers = []
    for d in range(1, count_x * count_y):
        other = lax.rem(plane_id + d, count_x * count_y)
        xy_peers.append({"gx": lax.div(other, count_y), "gy": lax.rem(other, count_y)})
    for peer in z_peers + xy_peers:
        pl.semaphore_signal(barrier, inc=1, device_id=peer, device_id_type=MESH)

    here = (gx, gx, gy, gy, gz, gz)
    counts = (count_x, count_x, count_y, count_y, count_z, count_z)
    present = [
        here[f] > 0 if f % 2 == 0 else here[f] < counts[f] - 1 for f in range(6)
    ]
    for f in range(6):

        @pl.when(jnp.logical_not(present[f]))
        def _():
            for e in range(4):
                faces[e, f] = jnp.zeros(faces.shape[2:], BF16)

    def face_copy(e, f):
        step = 1 if f % 2 else -1
        axis = AXES[f // 2]
        return pltpu.make_async_remote_copy(
            src_ref=send_faces.at[e, f],
            dst_ref=faces.at[e, f ^ 1],
            send_sem=face_send.at[e, f],
            recv_sem=face_recv.at[e, f ^ 1],
            device_id={axis: here[f] + step},
            device_id_type=MESH,
        )

    def face_arrival(e, f):
        return pltpu.make_async_remote_copy(
            src_ref=send_faces.at[e, f],
            dst_ref=faces.at[e, f],
            send_sem=face_send.at[e, f],
            recv_sem=face_recv.at[e, f],
            device_id={AXES[f // 2]: here[f]},
            device_id_type=MESH,
        )

    def pack_faces(e, field):
        for f in range(6):
            for c in range(comps):
                base = c * slab
                if f < 2:
                    x = 0 if f == 0 else cx - 1
                    piece = field[pl.ds(base + x * plane, plane), :]
                elif f < 4:
                    y = 0 if f == 2 else cy - 1
                    piece = jnp.concatenate(
                        [field[pl.ds(base + x * plane + y * cz, cz), :] for x in range(cx)], axis=0
                    )
                else:
                    z = 0 if f == 4 else cz - 1
                    piece = field[pl.ds(base + z, cx * cy, stride=cz), :]
                send_faces[e, f, pl.ds(c * plane, plane), :] = piece.astype(BF16)

            @pl.when(present[f])
            def _():
                face_copy(e, f).start()

    def wait_faces(e):
        for f in range(6):

            @pl.when(present[f])
            def _():
                face_arrival(e, f).wait_recv()

    def coarse_stages(k):
        def copy(view, peer, number):
            return pltpu.make_async_remote_copy(
                src_ref=view,
                dst_ref=view,
                send_sem=coarse_send.at[k, number],
                recv_sem=coarse_recv.at[k, number],
                device_id=peer,
                device_id_type=MESH,
            )

        stages, number = [], 0
        plan = [
            (coarse.at[k, gx, gy_high, gy_low, gz], z_peers),
            (coarse.at[k, gx, gy_high, gy_low], [(lambda o: {"gx": lax.div(o, high_count), "gy": lax.rem(o, high_count) * low_count + gy_low})(lax.rem(gx * high_count + gy_high + d, count_x * high_count)) for d in range(1, count_x * high_count)]),
            (coarse.at[k, :, :, gy_low], [{"gy": gy_high * low_count + lax.rem(gy_low + d, low_count)} for d in range(1, low_count)]),
        ]
        for view, peers in plan:
            stage = []
            for peer in peers:
                stage.append(copy(view, peer, number))
                number += 1
            stages.append(stage)
        return stages

    def start(stage):
        for copy in stage:
            copy.start()

    def arrive(stage):
        for copy in stage:
            copy.wait_recv()

    every_stage = []

    def prepare():
        eye = lax.broadcasted_iota(jnp.int32, (cz, cz), 0) == lax.broadcasted_iota(
            jnp.int32, (cz, cz), 1
        )

        def fill(i, carry):
            tile = stiff_ref[i]
            for y in range(cy):
                line = jnp.sum(jnp.where(eye, tile[y : y + 1, :], 0.0), axis=1, keepdims=True)
                start = pl.multiple_of(i * plane + y * cz, cz)
                diagonal[pl.ds(start, cz), :] = jnp.broadcast_to(line + 6.0, (cz, right.shape[1]))
            return carry

        lax.fori_loop(0, comps * cx, fill, 0)

        margin = margin_ref[...]
        for f in range(6):
            for c in range(comps):
                ids = lax.broadcasted_iota(jnp.int32, (plane, margin.shape[1]), 0) + (
                    (c * 6 + f) * plane
                )
                onehot[pl.ds((f * comps + c) * plane, plane), :] = jnp.where(
                    ids == margin, 1.0, 0.0
                ).astype(BF16)
        placed_turned[...] = placed_basis[...].astype(F32).T.astype(BF16)

    def precondition(k, e, field):
        residual = dot(placed_basis[...], own[...]).astype(BF16)
        coarse[k, gx, gy_high, gy_low, gz] = residual
        stages = coarse_stages(k)
        every_stage.extend(stages)
        if k == 0:
            pl.semaphore_wait(barrier, len(z_peers) + len(xy_peers))
        start(stages[0])
        pack_faces(e, field)
        if k == 0:
            prepare()
        else:
            add_products(0)
        for i in range(own_blocks):
            if k == 0:
                factor_loads[i].wait()
            values = dot(
                factor[pl.ds(i * blk, blk), pl.ds(0, (i + 1) * blk)],
                own[pl.ds(0, (i + 1) * blk), :],
            )
            front[:, pl.ds(i * blk, blk)] = values.T.astype(BF16)
            if i == own_blocks // 2 - 1:
                arrive(stages[0])
                start(stages[1])
        if k == 0:
            for i in range(own_blocks, all_blocks):
                factor_loads[i].wait()
                wide = (i + 1) * blk - rows
                face_factor[pl.ds(i * blk - rows, blk), :] = lax.dot_general(
                    factor[pl.ds(i * blk, blk), pl.ds(rows, wide)],
                    onehot[:, pl.ds(0, wide)],
                    (((1,), (1,)), ((), ())),
                    preferred_element_type=F32,
                ).astype(BF16)
        wait_faces(e)
        margin_faces = faces[e].reshape(-1, faces.shape[-1])
        for i in range(own_blocks, all_blocks):
            values = dot(factor[pl.ds(i * blk, blk), pl.ds(0, rows)], own[...]) + dot(
                face_factor[pl.ds(i * blk - rows, blk), :], margin_faces
            )
            front[:, pl.ds(i * blk, blk)] = values.T.astype(BF16)
        for j in range(own_blocks):
            cut = pl.ds(j * blk, blk)
            back[cut, :] = dot(
                front[:, pl.ds(j * blk, size - j * blk)], factor[pl.ds(j * blk, size - j * blk), cut]
            ).T
        if k == 0:
            loads[2].wait()
        arrive(stages[1])
        start(stages[2])
        arrive(stages[2])
        solved = dot(inverse[...], coarse[k].reshape(-1, coarse.shape[-1])).astype(BF16)
        search[k] = back[...] + dot(placed_turned[...], solved)

    def shaped(values):
        return values.reshape(cy, cz, -1)

    def operate(k, e):
        zi = lax.broadcasted_iota(jnp.int32, (cy, cz, right.shape[1]), 1)
        nothing = jnp.zeros((1, cz, right.shape[1]), F32)
        result = images.at[k]
        for c in range(comps):
            base = c * slab
            for x in range(cx):
                at = pl.ds(base + x * plane, plane)
                center = shaped(search[k, at, :])
                beside = jnp.concatenate([nothing, center[:-1]], axis=0)
                beside += jnp.concatenate([center[1:], nothing], axis=0)
                beside += jnp.where(zi == 0, 0.0, pltpu.roll(center, 1, axis=1))
                beside += jnp.where(zi == cz - 1, 0.0, pltpu.roll(center, cz - 1, axis=1))
                if x:
                    beside += shaped(search[k, pl.ds(base + (x - 1) * plane, plane), :])
                if x < cx - 1:
                    beside += shaped(search[k, pl.ds(base + (x + 1) * plane, plane), :])
                out = shaped(diagonal[at, :]) * center - beside
                result[at, :] = out.reshape(plane, -1)
        wait_faces(e)
        for c in range(comps):
            base = c * slab
            cut = pl.ds(c * plane, plane)
            x_low, x_high, y_low, y_high, z_low, z_high = (
                faces[e, f, cut, :].astype(F32) for f in range(6)
            )
            for z, piece in ((0, z_low), (cz - 1, z_high)):
                result[pl.ds(base + z, cx * cy, stride=cz), :] -= piece
            for x, piece in ((0, x_low), (cx - 1, x_high)):
                result[pl.ds(base + x * plane, plane), :] -= piece
            for y, piece in ((0, y_low), (cy - 1, y_high)):
                for x in range(cx):
                    result[pl.ds(base + x * plane + y * cz, cz), :] -= piece[x * cz : (x + 1) * cz]
        if k == 0:
            own[...] = result[...].astype(BF16)

    def add_products(k):
        totals = None
        for i in range(comps * cx):
            at = pl.ds(i * plane, plane)
            given, first = right[at, :], images[0, at, :]
            if k == 0:
                terms = [given * given, first * given, first * first]
            else:
                second = images[1, at, :]
                terms = [second * given, second * first, second * second]
            terms = [jnp.sum(shaped(term), axis=0) for term in terms]
            totals = terms if totals is None else [a + b for a, b in zip(totals, terms)]
        for q, total in enumerate(totals):
            sums_z[gz, pl.ds(k * 3 + q, 1), :] = jnp.sum(total, axis=0, keepdims=True)

    sums_z[gz] = jnp.zeros(sums_z.shape[1:], F32)
    loads[1].wait()
    ids = lax.broadcasted_iota(jnp.int32, (basis.shape[0], basis.shape[0]), 0)
    table = jnp.where(ids == map_ref[...], 1.0, 0.0).astype(BF16)
    placed_basis[...] = dot(table, basis[...]).astype(BF16)
    loads[0].wait()
    own[...] = right[...].astype(BF16)
    outs = [
        pltpu.make_async_copy(search.at[k], target, out_sem.at[k])
        for k, target in enumerate((search_one_hbm, search_two_hbm))
    ]
    precondition(0, 0, right)
    pack_faces(1, search.at[0])
    outs[0].start()
    operate(0, 1)
    precondition(1, 2, images.at[0])
    pack_faces(3, search.at[1])
    outs[1].start()
    operate(1, 3)
    add_products(1)

    sum_copies = []

    def share(slots, index, peers, base):
        copies = []
        for n, peer in enumerate(peers):
            copies.append(
                pltpu.make_async_remote_copy(
                    src_ref=slots.at[index],
                    dst_ref=slots.at[index],
                    send_sem=sum_send.at[base + n],
                    recv_sem=sum_recv.at[base + n],
                    device_id=peer,
                    device_id_type=MESH,
                )
            )
        start(copies)
        arrive(copies)
        sum_copies.extend(copies)
        total = slots[0]
        for n in range(1, slots.shape[0]):
            total = total + slots[n]
        return total

    sums_xy[plane_id] = share(sums_z, gz, z_peers, 0)
    total = share(sums_xy, plane_id, xy_peers, len(z_peers))
    vv, iv, ii, tv, ti, tt = (total[q : q + 1] for q in range(6))

    start_square = vv + EPSILON
    start_norm = jnp.sqrt(start_square)
    along_one = iv / start_square
    rest = jnp.maximum(
        ii / start_square - along_one * along_one * (2.0 - vv / start_square), 0.0
    )
    square_two = rest + EPSILON
    norm_two = jnp.sqrt(square_two)
    scale = start_norm * norm_two
    cross_two = (tv - along_one * iv) / (start_square * norm_two)
    along_two = (ti - along_one * ii - along_one * (tv - along_one * iv)) / (
        start_square * square_two
    )
    square_image = (tt - along_one * (2.0 * ti - along_one * ii)) / (start_square * square_two)
    overlap = (iv - along_one * vv) / (start_square * norm_two)
    rest = (
        square_image
        - cross_two * cross_two * (2.0 - vv / start_square)
        - along_two * along_two * (2.0 - rest / square_two)
        + 2.0 * cross_two * along_two * overlap
    )
    norm_three = jnp.sqrt(jnp.maximum(rest, 0.0) + EPSILON)
    radius_one = jnp.sqrt(along_one * along_one + square_two)
    cosine_one = along_one / radius_one
    sine_one = norm_two / radius_one
    turned_one = cosine_one * cross_two + sine_one * along_two
    turned_two = cosine_one * along_two - sine_one * cross_two
    radius_two = jnp.sqrt(turned_two * turned_two + norm_three * norm_three)
    cosine_two = turned_two / radius_two
    sine_two = norm_three / radius_two
    coef_two = -cosine_two * sine_one * start_norm / radius_two
    coef_one = (cosine_one * start_norm - turned_one * coef_two) / radius_one
    weight_two = coef_two / scale
    weight_one = coef_one / start_norm - along_one * weight_two
    weights_ref[0:1, :] = weight_one
    weights_ref[1:2, :] = weight_two
    weights_ref[2:3, :] = sine_one * sine_two
    for out in outs:
        out.wait()

    for stage in every_stage + [sum_copies]:
        for copy in stage:
            copy.wait_send()
    for e in range(4):
        for f in range(6):

            @pl.when(present[f])
            def _():
                face_copy(e, f).wait_send()


def combine(weights_ref, one_ref, two_ref, solution_ref, ratio_ref):
    solution_ref[...] = weights_ref[0:1, :] * one_ref[...] + weights_ref[1:2, :] * two_ref[...]
    ratio_ref[...] = weights_ref[2:3, :]


def local(dims, right_side, stiffness, local_factor, basis, coarse_map, margin_index, coarse_inverse):
    cells = right_side.shape[:4]
    comps, cx, cy, cz = cells
    rhs = right_side.shape[-1]
    rows = comps * cx * cy * cz
    size = local_factor.shape[-1]
    functions = basis.shape[-2]
    margin = margin_index.shape[-1]
    face = comps * cy * cz
    assert cx == cy == cz and rows % 256 == 0 and size % 256 == 0
    low_count = 2 if dims[1] % 2 == 0 else 1
    devices = dims[0] * dims[1] * dims[2]
    copies = dims[2] - 1 + dims[0] * dims[1] // low_count - 1 + low_count - 1
    sum_copies = dims[2] - 1 + dims[0] * dims[1] - 1
    anywhere = pl.BlockSpec(memory_space=pl.ANY)
    vmem = pl.BlockSpec(memory_space=pltpu.VMEM)
    search_one, search_two, weights = pl.pallas_call(
        functools.partial(kernel, dims, cells),
        out_shape=(
            jax.ShapeDtypeStruct((rows, rhs), F32),
            jax.ShapeDtypeStruct((rows, rhs), F32),
            jax.ShapeDtypeStruct((8, rhs), F32),
        ),
        in_specs=[anywhere, vmem, anywhere, anywhere, vmem, vmem, anywhere],
        out_specs=(anywhere, anywhere, vmem),
        scratch_shapes=[
            pltpu.VMEM((rows, rhs), F32),
            pltpu.VMEM((size, size), BF16),
            pltpu.VMEM((functions, rows), BF16),
            pltpu.VMEM(coarse_inverse.shape, BF16),
            pltpu.VMEM((rows, rhs), BF16),
            pltpu.VMEM((functions, rows), BF16),
            pltpu.VMEM((rows, functions), BF16),
            pltpu.VMEM((6 * face, margin), BF16),
            pltpu.VMEM((margin, 6 * face), BF16),
            pltpu.VMEM((rows, rhs), F32),
            pltpu.VMEM((2, rows, rhs), F32),
            pltpu.VMEM((2, rows, rhs), F32),
            pltpu.VMEM((rhs, size), BF16),
            pltpu.VMEM((rows, rhs), F32),
            pltpu.VMEM((4, 6, face, rhs), BF16),
            pltpu.VMEM((4, 6, face, rhs), BF16),
            pltpu.VMEM(
                (2, dims[0], dims[1] // low_count, low_count, dims[2], functions, rhs), BF16
            ),
            pltpu.VMEM((dims[2], 8, rhs), F32),
            pltpu.VMEM((dims[0] * dims[1], 8, rhs), F32),
            pltpu.SemaphoreType.DMA((3,)),
            pltpu.SemaphoreType.DMA((size // 256,)),
            pltpu.SemaphoreType.DMA((4, 6)),
            pltpu.SemaphoreType.DMA((4, 6)),
            pltpu.SemaphoreType.DMA((2, copies)),
            pltpu.SemaphoreType.DMA((2, copies)),
            pltpu.SemaphoreType.DMA((sum_copies,)),
            pltpu.SemaphoreType.DMA((sum_copies,)),
            pltpu.SemaphoreType.DMA((2,)),
        ],
        compiler_params=pltpu.CompilerParams(
            collective_id=0, has_side_effects=True, vmem_limit_bytes=56 * 1024 * 1024
        ),
    )(
        right_side.reshape(rows, rhs),
        stiffness.reshape(comps * cx, cy, cz),
        local_factor.reshape(size, size),
        basis.reshape(functions, rows),
        coarse_map.reshape(1, functions),
        margin_index.reshape(1, margin),
        coarse_inverse,
    )
    parts = 2
    block = pl.BlockSpec((rows // parts, rhs), lambda i: (i, 0))
    solved, ratio = pl.pallas_call(
        combine,
        grid=(parts,),
        out_shape=(
            jax.ShapeDtypeStruct((rows, rhs), F32),
            jax.ShapeDtypeStruct((1, rhs), F32),
        ),
        in_specs=[pl.BlockSpec((8, rhs), lambda i: (0, 0)), block, block],
        out_specs=(block, pl.BlockSpec((1, rhs), lambda i: (0, 0))),
    )(weights, search_one, search_two)
    return solved.reshape(right_side.shape), ratio.reshape(rhs)


def solution(mesh):
    dims = tuple(mesh.shape[axis] for axis in AXES)
    return jax.shard_map(
        functools.partial(local, dims),
        mesh=mesh,
        in_specs=(
            P(None, "gx", "gy", "gz", None),
            P(None, "gx", "gy", "gz"),
            P("gx", "gy", "gz", None, None),
            P("gx", "gy", "gz", None, None),
            P("gx", "gy", "gz", None),
            P("gx", "gy", "gz", None),
            P(("gx", "gy", "gz"), None),
        ),
        out_specs=(P(None, "gx", "gy", "gz", None), P()),
        check_vma=False,
    )
```
